512 devices in a mesh: ctx: 64 (over y, x, z_hi), head: 8 (over z_lo, core).
Axes of the slice: x: 4, y: 8, z: 8 (z_hi: 2, z_lo: 4; z = z_hi * 4 + z_lo), core: 2. Of those that a mesh axis runs over, the one named last changes fastest.
Arguments:
- qkv: bfloat16 [32768, 3, 512], P(('ctx', 'head')), may hold values from -10 to 10
- w_out: bfloat16 [512, 1024], replicated, may hold values from -0.25 to 0.25
Outputs:
- mixed: bfloat16 [32768, 1024], P(('ctx', 'head'))
The draws below stay inside these ranges and needn't reach their ends.
All inputs are finite; a program needn't handle non-finite values.
Results may differ from the reference program's by a relative error of at most 0.0095.
Values may be sent and summed in bfloat16 or wider, within the bound.
A program may use at most 64 MiB of HBM per device.

```python
import jax
import jax.numpy as jnp
from jax import lax

D = 1024
HEADS = 8
DH = 64
FRAMES = 32768
HD = 512


def draw_qkv(key, part):
    key = jax.random.fold_in(key, 11)
    first_key = jax.random.fold_in(key, 0)
    shape = (FRAMES, 3, HEADS * DH)
    scaling = jnp.array([2.5, 1.0, 4.0], jnp.float32).reshape(1, 3, 1)
    result = jax.random.normal(first_key, shape, jnp.float32) * scaling
    return jnp.clip(result, -10.0, 10.0).astype(jnp.bfloat16)


def bell_draw(stream_key, shape, scale, most, dtype=jnp.bfloat16):
    return jnp.clip(scale * jax.random.normal(stream_key, shape, jnp.float32), -most, most).astype(dtype)


def setup_inputs(seed: int = 0) -> dict:
    seeds = jax.random.split(jax.random.key(seed), 3)
    return {
        "qkv": draw_qkv(jax.random.fold_in(seeds[2], 71), 0),
        "w_out": bell_draw(seeds[1], (HD, D), HD ** -0.5, 0.25),
    }


def attend_head(operands):
    queries, keys, values = operands
    rows = min(2048, FRAMES)

    def per_block(query_block):
        scores = jnp.dot(query_block, keys.T, preferred_element_type=jnp.float32) * (DH ** -0.5)
        highest = jnp.max(scores, axis=1, keepdims=True)
        weights = jnp.exp(scores - highest)
        totals = jnp.sum(weights, axis=1, keepdims=True)
        product = jnp.dot(weights.astype(jnp.bfloat16), values, preferred_element_type=jnp.float32)
        return product / totals

    blocks = queries.reshape(FRAMES // rows, rows, DH)
    return lax.map(per_block, blocks).reshape(FRAMES, DH)


def reference(qkv, w_out):
    stacked = qkv.reshape(FRAMES, 3, HEADS, DH).transpose(1, 2, 0, 3)
    attended = lax.map(attend_head, (stacked[0], stacked[1], stacked[2]))
    attended = attended.astype(jnp.bfloat16).transpose(1, 0, 2).reshape(FRAMES, HEADS * DH)
    return jnp.dot(attended, w_out, preferred_element_type=jnp.float32).astype(jnp.bfloat16)
```

```python
import functools

import jax
import jax.numpy as jnp
from jax import lax
from jax.experimental import pallas as pl
from jax.experimental.pallas import tpu as pltpu
from jax.sharding import PartitionSpec as P

MESH = pl.DeviceIdType.MESH
F32 = jnp.float32
BF16 = jnp.bfloat16
LOG2E = 1.4426950408889634

KEY_LEFT = ((0, 1), (1, 3), (3, 5), (5, 7))
KEY_RIGHT = ((0, 2), (2, 4), (4, 6), (6, 7))


def dot(a, b):
    return jnp.dot(a, b, preferred_element_type=F32)


def device(y, x, z, c):
    return ((y * 4 + x) * 2 + z // 4, (z % 4) * 2 + c)


def kernel(
    qkv_ref, w_hbm, out_ref,
    pieces, grouped, keys, values, queries, stationary, total, highest,
    part_out, stat_out, part_in, stat_in, back_out, back_in, w_vmem, rows,
    a2a_s, a2a_r, kv_s, kv_r, q_s, q_r, po_s, po_r, bk_s, bk_r, w_sem,
):
    ctx, head = lax.axis_index("ctx"), lax.axis_index("head")
    y, x, z, c = ctx // 8, (ctx // 2) % 4, (ctx % 2) * 4 + head // 2, head % 2

    def y_peer(k):
        return device((y + k) % 8, x, z, c)

    def xc_peer(n):
        pair = n // 2
        dx = pair + pair // 2 - 2 * (pair // 3)
        return device(y, (x + dx) % 4, z, (c + n % 2) % 2)

    def inverse(n):
        pair = n // 2
        return 2 * ((2 * pair) % 3 + 3 * (pair // 3)) + n % 2

    left, right = device(y, x, (z + 7) % 8, c), device(y, x, (z + 1) % 8, c)

    barrier = pltpu.get_barrier_semaphore()
    partners = [y_peer(k) for k in range(1, 8)] + [xc_peer(n) for n in range(1, 8)] + [left, right]
    for partner in partners:
        pl.semaphore_signal(barrier, inc=1, device_id=partner, device_id_type=MESH)

    w_copy = pltpu.make_async_copy(w_hbm, w_vmem, w_sem)
    w_copy.start()

    for t in range(3):
        rows[t] = qkv_ref[:, t, :]
        for h in range(8):
            cut = rows[t, :, 64 * h : 64 * h + 64]
            pieces[h, t] = jnp.concatenate([cut[:32], cut[32:]], axis=1)
    for n in range(8):
        values[n, :, 64:80, :] = jnp.ones((2, 16, 256), BF16)
    for i in range(16):
        stationary[i, 0, 64:, :] = jnp.zeros((64, 256), BF16)
        stationary[i, 1, :64, :] = jnp.zeros((64, 256), BF16)

    pl.semaphore_wait(barrier, len(partners))

    def spread(k, first, count, part):
        there = (y + k) % 8
        return pltpu.make_async_remote_copy(
            src_ref=pieces.at[there, pl.ds(first, count)],
            dst_ref=grouped.at[pl.ds(first, count), y],
            send_sem=a2a_s.at[k, part],
            recv_sem=a2a_r.at[k, part],
            device_id=y_peer(k),
            device_id_type=MESH,
        )

    kv_spread = [spread(k, 1, 2, 0) for k in (4, 3, 5, 2, 6, 1, 7)]
    q_spread = [spread(k, 0, 1, 1) for k in (4, 3, 5, 2, 6, 1, 7)]
    for copy in kv_spread + q_spread:
        copy.start()
    for t in range(3):
        grouped[t, y] = pieces[y, t]
    started = kv_spread + q_spread

    def send_keys(step, direction, keys_too, values_too):
        here, there = (KEY_LEFT, KEY_RIGHT)[direction][step]
        copies = []
        for part, ref, wanted in ((0, keys, keys_too), (1, values, values_too)):
            if wanted:
                cut = (lambda n: ref.at[n]) if part == 0 else (lambda n: ref.at[n, :, pl.ds(0, 64)])
                copies.append(
                    pltpu.make_async_remote_copy(
                        src_ref=cut(here),
                        dst_ref=cut(there),
                        send_sem=kv_s.at[step, direction, part],
                        recv_sem=kv_r.at[there, part],
                        device_id=(left, right)[direction],
                        device_id_type=MESH,
                    )
                )
        for copy in copies:
            copy.start()
        started.extend(copies)
        return copies

    for copy in kv_spread:
        copy.wait_recv()
    keys[0] = grouped[1].reshape(256, 128)
    turned = grouped[2].reshape(256, 128).astype(F32).T.astype(BF16)
    values[0, 0, :64] = turned[:64]
    values[0, 1, :64] = turned[64:]
    arriving = [send_keys(0, 0, True, True), send_keys(0, 1, True, True)]

    for copy in q_spread:
        copy.wait_recv()
    queries[0] = (grouped[0].reshape(256, 128).astype(F32) * 0.125).T.astype(BF16)

    q_copies = {}
    for n in (1, 2, 4, 3, 5, 6, 7):
        q_copies[n] = pltpu.make_async_remote_copy(
            src_ref=queries.at[0],
            dst_ref=queries.at[inverse(n)],
            send_sem=q_s.at[n],
            recv_sem=q_r.at[inverse(n)],
            device_id=xc_peer(n),
            device_id_type=MESH,
        )
        q_copies[n].start()
        started.append(q_copies[n])

    def take_queries(n):
        if n:
            q_copies[inverse(n)].wait_recv()
        for t in range(2):
            half = queries[n, 64 * t : 64 * t + 64, :]
            stationary[2 * n + t, 0, :64, :] = half
            stationary[2 * n + t, 1, 64:, :] = half

    def take_keys(step):
        nonlocal arriving
        for copies in arriving:
            for copy in copies:
                copy.wait_recv()
        if step < 3:
            last = step == 2
            arriving = [send_keys(step + 1, 0, True, not last), send_keys(step + 1, 1, not last, True)]

    def scores(i, n):
        found, top = [], []
        for t in range(2):
            pair = [dot(keys[n], stationary[2 * i + t, h]) * LOG2E for h in range(2)]
            top.append(jnp.maximum(*[jnp.max(s.reshape(32, 8, 256), axis=0) for s in pair]))
            found.append(pair)
        return found, top

    def weigh(i, n, found, top, first):
        for t in range(2):
            newest = jnp.max(top[t], axis=0, keepdims=True)
            if not first:
                before = highest[2 * i + t][:1]
                newest = jnp.maximum(before, newest)
                factor = jnp.exp2(before - newest)
            highest[2 * i + t] = jnp.broadcast_to(newest, (8, 256))
            added = sum(dot(values[n, h], jnp.exp2(found[t][h] - newest).astype(BF16)) for h in range(2))
            total[2 * i + t] = added if first else total[2 * i + t] * factor + added

    def attend(units):
        held = []
        for i, n, first in units:
            held.append((i, n, *scores(i, n), first))
            if len(held) > 1:
                weigh(*held.pop(0))
        weigh(*held.pop(0))

    take_queries(0)
    attend([(0, 0, True)])
    take_queries(1)
    attend([(1, 0, True)])
    take_keys(0)
    attend([(i, n, False) for i in (0, 1) for n in (1, 2)])
    take_queries(2)
    take_queries(3)

    @pl.loop(2, 4)
    def _(i):
        attend([(i, n, n == 0) for n in range(3)])

    take_keys(1)

    @pl.loop(0, 2)
    def _(i):
        attend([(2 * i + k, n, False) for k in (0, 1) for n in (3, 4)])

    take_queries(4)
    take_queries(5)

    @pl.loop(4, 6)
    def _(i):
        attend([(i, n, n == 0) for n in range(5)])

    take_keys(2)
    take_queries(6)
    take_queries(7)

    @pl.loop(6, 8)
    def _(i):
        attend([(i, n, n == 0) for n in range(5)])

    take_keys(3)

    def give_back(n):
        there = inverse(n)
        pairs = ((part_out, part_in), (stat_out, stat_in))
        return [
            pltpu.make_async_remote_copy(
                src_ref=mine.at[n],
                dst_ref=theirs.at[there],
                send_sem=po_s.at[n, k],
                recv_sem=po_r.at[there, k],
                device_id=xc_peer(n),
                device_id_type=MESH,
            )
            for k, (mine, theirs) in enumerate(pairs)
        ]

    @pl.loop(0, 8)
    def _(j):
        i = 7 - j
        attend([(i, n, False) for n in (5, 6, 7)])
        for t in range(2):
            whole = total[2 * i + t]
            sums = whole[64:65]
            part_out[i, 64 * t : 64 * t + 64, :] = (whole[:64] * (1.0 / sums)).astype(BF16)
            stat_out[i, 4 * t : 4 * t + 4, :] = jnp.broadcast_to(highest[2 * i + t][:1] + jnp.log2(sums), (4, 256))

        @pl.when(i != 0)
        def _():
            for copy in give_back(i):
                copy.start()

    for n in range(1, 8):
        for copy in give_back(inverse(n)):
            copy.wait_recv()
    mixed = []
    for t in range(2):
        stats = [stat_out[0, 4 * t : 4 * t + 1, :]] + [stat_in[n, 4 * t : 4 * t + 1, :] for n in range(1, 8)]
        top = functools.reduce(jnp.maximum, stats)
        shares = [jnp.exp2(s - top) for s in stats]
        scale = 1.0 / sum(shares)
        piece = [part_out[0, 64 * t : 64 * t + 64, :]] + [part_in[n, 64 * t : 64 * t + 64, :] for n in range(1, 8)]
        mixed.append(sum(p.astype(F32) * (s * scale) for p, s in zip(piece, shares)))
    back_out[...] = jnp.concatenate(mixed, axis=0).T.astype(BF16).reshape(8, 32, 128)

    returns = []
    for k in (4, 3, 5, 2, 6, 1, 7):
        copy = pltpu.make_async_remote_copy(
            src_ref=back_out.at[(y + k) % 8],
            dst_ref=back_in.at[y],
            send_sem=bk_s.at[k],
            recv_sem=bk_r.at[k],
            device_id=y_peer(k),
            device_id_type=MESH,
        )
        copy.start()
        returns.append(copy)
    back_in[y] = back_out[y]
    w_copy.wait()
    for copy in started:
        copy.wait_send()
    for n in range(1, 8):
        for copy in give_back(n):
            copy.wait_send()
    for copy in returns:
        copy.wait_recv()
    halves = [jnp.concatenate([back_in[h][:, 64 * t : 64 * t + 64] for h in range(8)], axis=1) for t in range(2)]
    out_ref[...] = dot(jnp.concatenate(halves, axis=0), w_vmem[...]).astype(BF16)
    for copy in returns:
        copy.wait_send()


def body(qkv, w_out):
    dma = pltpu.SemaphoreType.DMA
    return pl.pallas_call(
        kernel,
        out_shape=jax.ShapeDtypeStruct((64, 1024), BF16),
        in_specs=[pl.BlockSpec(memory_space=pltpu.VMEM), pl.BlockSpec(memory_space=pl.ANY)],
        out_specs=pl.BlockSpec(memory_space=pltpu.VMEM),
        scratch_shapes=[
            pltpu.VMEM((8, 3, 32, 128), BF16),
            pltpu.VMEM((3, 8, 32, 128), BF16),
            pltpu.VMEM((8, 256, 128), BF16),
            pltpu.VMEM((8, 2, 80, 256), BF16),
            pltpu.VMEM((8, 128, 256), BF16),
            pltpu.VMEM((16, 2, 128, 256), BF16),
            pltpu.VMEM((16, 80, 256), F32),
            pltpu.VMEM((16, 8, 256), F32),
            pltpu.VMEM((8, 128, 256), BF16),
            pltpu.VMEM((8, 8, 256), F32),
            pltpu.VMEM((8, 128, 256), BF16),
            pltpu.VMEM((8, 8, 256), F32),
            pltpu.VMEM((8, 32, 128), BF16),
            pltpu.VMEM((8, 32, 128), BF16),
            pltpu.VMEM((512, 1024), BF16),
            pltpu.VMEM((3, 64, 512), BF16),
            dma((8, 2)), dma((8, 2)),
            dma((4, 2, 2)), dma((8, 2)),
            dma((8,)), dma((8,)),
            dma((8, 2)), dma((8, 2)),
            dma((8,)), dma((8,)),
            dma,
        ],
        compiler_params=pltpu.CompilerParams(collective_id=0, has_side_effects=True, vmem_limit_bytes=56 << 20),
    )(qkv, w_out)


def solution(mesh):
    return jax.shard_map(
        body,
        mesh=mesh,
        in_specs=(P(("ctx", "head"), None, None), P()),
        out_specs=P(("ctx", "head"), None),
        check_vma=False,
    )
```

```python
import functools

import jax
import jax.numpy as jnp
from jax import lax
from jax.experimental import pallas as pl
from jax.experimental.pallas import tpu as pltpu
from jax.sharding import PartitionSpec as P

MESH = pl.DeviceIdType.MESH
F32 = jnp.float32
BF16 = jnp.bfloat16
LOG2E = 1.4426950408889634

KEY_LEFT = ((0, 1), (1, 3), (3, 5), (5, 7))
KEY_RIGHT = ((0, 2), (2, 4), (4, 6), (6, 7))


def dot(a, b):
    return jnp.dot(a, b, preferred_element_type=F32)


def device(y, x, z, c):
    return ((y * 4 + x) * 2 + z // 4, (z % 4) * 2 + c)


def kernel(
    qkv_hbm, out_ref,
    qkv_ref, pieces, grouped, keys, doubled, values, queries, stationary, total, highest,
    part_out, stat_out, part_in, stat_in, back_out, back_in,
    a2a_s, a2a_r, kv_s, kv_r, q_s, q_r, po_s, po_r, bk_s, bk_r, in_sem,
):
    ctx, head = lax.axis_index("ctx"), lax.axis_index("head")
    y, x, z, c = ctx // 8, (ctx // 2) % 4, (ctx % 2) * 4 + head // 2, head % 2

    def y_peer(k):
        return device((y + k) % 8, x, z, c)

    def xc_peer(n):
        pair = n // 2
        dx = pair + pair // 2 - 2 * (pair // 3)
        return device(y, (x + dx) % 4, z, (c + n % 2) % 2)

    def inverse(n):
        pair = n // 2
        return 2 * ((2 * pair) % 3 + 3 * (pair // 3)) + n % 2

    left, right = device(y, x, (z + 7) % 8, c), device(y, x, (z + 1) % 8, c)

    barrier = pltpu.get_barrier_semaphore()
    partners = [y_peer(k) for k in range(1, 8)] + [xc_peer(n) for n in range(1, 8)] + [left, right]
    for partner in partners:
        pl.semaphore_signal(barrier, inc=1, device_id=partner, device_id_type=MESH)

    fetch = pltpu.make_async_copy(qkv_hbm, qkv_ref, in_sem)
    fetch.start()
    fetch.wait()

    for t in (1, 2, 0):
        for h in range(8):
            cut = qkv_ref[t, :, 64 * h : 64 * h + 64]
            pieces[h, t] = jnp.concatenate([cut[:32], cut[32:]], axis=1)

    pl.semaphore_wait(barrier, len(partners))

    def spread(k, first, count, part):
        there = (y + k) % 8
        return pltpu.make_async_remote_copy(
            src_ref=pieces.at[there, pl.ds(first, count)],
            dst_ref=grouped.at[pl.ds(first, count), y],
            send_sem=a2a_s.at[k, part],
            recv_sem=a2a_r.at[k, part],
            device_id=y_peer(k),
            device_id_type=MESH,
        )

    kv_spread = [spread(k, 1, 2, 0) for k in (4, 3, 5, 2, 6, 1, 7)]
    q_spread = [spread(k, 0, 1, 1) for k in (4, 3, 5, 2, 6, 1, 7)]
    for copy in kv_spread + q_spread:
        copy.start()
    for t in range(3):
        grouped[t, y] = pieces[y, t]
    for n in range(8):
        values[n, :, 64:80, :] = jnp.ones((2, 16, 256), BF16)
    started = kv_spread + q_spread

    def send_keys(step, part):
        copies = []
        for direction in range(2):
            if step < 3 or direction == part:
                here, there = (KEY_LEFT, KEY_RIGHT)[direction][step]
                ref = (keys, values)[part]
                place = (lambda n: ref.at[n]) if part == 0 else (lambda n: ref.at[n, :, pl.ds(0, 64)])
                copies.append(
                    pltpu.make_async_remote_copy(
                        src_ref=place(here),
                        dst_ref=place(there),
                        send_sem=kv_s.at[step, direction, part],
                        recv_sem=kv_r.at[there, part],
                        device_id=(left, right)[direction],
                        device_id_type=MESH,
                    )
                )
        for copy in copies:
            copy.start()
        started.extend(copies)
        arriving[step, part] = copies

    arriving = {}

    def double_keys(n):
        both = keys[n]
        for h in range(2):
            one = both[:, 64 * h : 64 * h + 64]
            doubled[n, h] = jnp.concatenate([one, one], axis=1)

    def take_keys(step, part):
        for copy in arriving[step, part]:
            copy.wait_recv()
        if step < 3:
            send_keys(step + 1, part)
        if part == 0:
            for n in (1 + 2 * step, 2 + 2 * step)[: 2 if step < 3 else 1]:
                double_keys(n)

    for copy in kv_spread:
        copy.wait_recv()
    keys[0] = grouped[1].reshape(256, 128)
    send_keys(0, 0)
    turned = grouped[2].reshape(256, 128).astype(F32).T.astype(BF16)
    values[0, 0, :64] = turned[:64]
    values[0, 1, :64] = turned[64:]
    send_keys(0, 1)
    double_keys(0)

    for copy in q_spread:
        copy.wait_recv()
    queries[0] = grouped[0].reshape(256, 128).astype(F32).T.astype(BF16)

    q_copies = {}
    for n in (1, 2, 4, 3, 5, 6, 7):
        q_copies[n] = pltpu.make_async_remote_copy(
            src_ref=queries.at[0],
            dst_ref=queries.at[inverse(n)],
            send_sem=q_s.at[n],
            recv_sem=q_r.at[inverse(n)],
            device_id=xc_peer(n),
            device_id_type=MESH,
        )
        q_copies[n].start()
        started.append(q_copies[n])

    def take_queries(n):
        if n:
            q_copies[inverse(n)].wait_recv()
        scaled = queries[n].astype(F32) * (LOG2E / 8)
        high = scaled.astype(BF16)
        low = (scaled - high.astype(F32)).astype(BF16)
        for t in range(2):
            stationary[2 * n + t, :64, :] = high[64 * t : 64 * t + 64]
            stationary[2 * n + t, 64:, :] = low[64 * t : 64 * t + 64]

    def scores(i, n, h):
        found = [dot(doubled[n, h], stationary[2 * i + t]) for t in range(2)]
        return found, [jnp.max(s.reshape(32, 8, 256), axis=0) for s in found]

    def weigh(i, n, h, found, top):
        for t in range(2):
            newest = jnp.max(top[t], axis=0, keepdims=True)
            first = n == 0 and h == 0
            if not first:
                before = highest[2 * i + t][:1]
                newest = jnp.maximum(before, newest)
                factor = jnp.exp2(before - newest)
            highest[2 * i + t] = jnp.broadcast_to(newest, (8, 256))
            added = dot(values[n, h], jnp.exp2(found[t] - newest).astype(BF16))
            total[2 * i + t] = added if first else total[2 * i + t] * factor + added

    def attend(chunks, slots):
        held = []
        for i in chunks:
            for n in slots:
                for h in range(2):
                    held.append((i, n, h, *scores(i, n, h)))
                    if len(held) > 2:
                        weigh(*held.pop(0))
        for unit in held:
            weigh(*unit)

    take_queries(0)
    attend((0,), (0,))
    take_queries(1)
    attend((1,), (0,))
    take_keys(0, 0)
    take_keys(0, 1)
    attend((0, 1), (1, 2))
    take_queries(2)
    take_queries(4)
    attend((2, 4), (0, 1, 2))
    take_keys(1, 0)
    take_queries(3)
    take_queries(5)
    take_keys(1, 1)
    attend((3, 5), (0, 1, 2))

    attend((0, 1, 2, 3), (3, 4))
    take_keys(2, 0)
    take_queries(6)
    take_queries(7)
    attend((4, 5), (3, 4))
    take_keys(2, 1)
    attend((6, 7), (0, 1, 2, 3, 4))
    take_keys(3, 0)
    take_keys(3, 1)

    def give_back(n):
        there = inverse(n)
        pairs = ((part_out, part_in), (stat_out, stat_in))
        return [
            pltpu.make_async_remote_copy(
                src_ref=mine.at[n],
                dst_ref=theirs.at[there],
                send_sem=po_s.at[n, k],
                recv_sem=po_r.at[there, k],
                device_id=xc_peer(n),
                device_id_type=MESH,
            )
            for k, (mine, theirs) in enumerate(pairs)
        ]

    @pl.loop(0, 4)
    def _(k):
        first = 6 - 2 * k
        attend((first, first + 1), (5, 6, 7))
        for i in (first, first + 1):
            for t in range(2):
                whole = total[2 * i + t]
                sums = whole[64:65]
                part_out[i, 64 * t : 64 * t + 64, :] = (whole[:64] * (1.0 / sums)).astype(BF16)
                stat_out[i, 4 * t : 4 * t + 4, :] = jnp.broadcast_to(highest[2 * i + t][:1] + jnp.log2(sums), (4, 256))

            @pl.when(i != 0)
            def _():
                for copy in give_back(i):
                    copy.start()

    for n in range(1, 8):
        for copy in give_back(inverse(n)):
            copy.wait_recv()
    mixed = []
    for t in range(2):
        stats = [stat_out[0, 4 * t : 4 * t + 1, :]] + [stat_in[n, 4 * t : 4 * t + 1, :] for n in range(1, 8)]
        top = functools.reduce(jnp.maximum, stats)
        shares = [jnp.exp2(s - top) for s in stats]
        scale = 1.0 / sum(shares)
        piece = [part_out[0, 64 * t : 64 * t + 64, :]] + [part_in[n, 64 * t : 64 * t + 64, :] for n in range(1, 8)]
        mixed.append(sum(p.astype(F32) * (s * scale) for p, s in zip(piece, shares)))
    back_out[...] = jnp.concatenate(mixed, axis=0).T.astype(BF16).reshape(8, 32, 128)

    returns = []
    for k in (4, 3, 5, 2, 6, 1, 7):
        copy = pltpu.make_async_remote_copy(
            src_ref=back_out.at[(y + k) % 8],
            dst_ref=back_in.at[y],
            send_sem=bk_s.at[k],
            recv_sem=bk_r.at[k],
            device_id=y_peer(k),
            device_id_type=MESH,
        )
        copy.start()
        returns.append(copy)
    back_in[y] = back_out[y]
    for copy in started:
        copy.wait_send()
    for n in range(1, 8):
        for copy in give_back(n):
            copy.wait_send()
    for copy in returns:
        copy.wait_recv()
    for h in range(8):
        for t in range(2):
            out_ref[32 * t : 32 * t + 32, 64 * h : 64 * h + 64] = back_in[h][:, 64 * t : 64 * t + 64]
    for copy in returns:
        copy.wait_send()


def body(qkv, w_out):
    dma = pltpu.SemaphoreType.DMA
    attended = pl.pallas_call(
        kernel,
        out_shape=jax.ShapeDtypeStruct((64, 512), BF16),
        in_specs=[pl.BlockSpec(memory_space=pl.ANY)],
        out_specs=pl.BlockSpec(memory_space=pltpu.VMEM),
        scratch_shapes=[
            pltpu.VMEM((3, 64, 512), BF16),
            pltpu.VMEM((8, 3, 32, 128), BF16),
            pltpu.VMEM((3, 8, 32, 128), BF16),
            pltpu.VMEM((8, 256, 128), BF16),
            pltpu.VMEM((8, 2, 256, 128), BF16),
            pltpu.VMEM((8, 2, 80, 256), BF16),
            pltpu.VMEM((8, 128, 256), BF16),
            pltpu.VMEM((16, 128, 256), BF16),
            pltpu.VMEM((16, 80, 256), F32),
            pltpu.VMEM((16, 8, 256), F32),
            pltpu.VMEM((8, 128, 256), BF16),
            pltpu.VMEM((8, 8, 256), F32),
            pltpu.VMEM((8, 128, 256), BF16),
            pltpu.VMEM((8, 8, 256), F32),
            pltpu.VMEM((8, 32, 128), BF16),
            pltpu.VMEM((8, 32, 128), BF16),
            dma((8, 2)), dma((8, 2)),
            dma((4, 2, 2)), dma((8, 2)),
            dma((8,)), dma((8,)),
            dma((8, 2)), dma((8, 2)),
            dma((8,)), dma((8,)),
            dma,
        ],
        compiler_params=pltpu.CompilerParams(collective_id=0, has_side_effects=True, vmem_limit_bytes=56 << 20),
    )(qkv.transpose(1, 0, 2))
    return dot(attended, w_out).astype(BF16)


def solution(mesh):
    return jax.shard_map(
        body,
        mesh=mesh,
        in_specs=(P(("ctx", "head"), None, None), P()),
        out_specs=P(("ctx", "head"), None),
        check_vma=False,
    )
```

```python
import functools

import jax
import jax.numpy as jnp
from jax import lax
from jax.experimental import pallas as pl
from jax.experimental.pallas import tpu as pltpu
from jax.sharding import PartitionSpec as P

MESH = pl.DeviceIdType.MESH
F32 = jnp.float32
BF16 = jnp.bfloat16
LOG2E = 1.4426950408889634

KEY_LEFT = ((0, 1), (1, 3), (3, 5), (5, 7))
KEY_RIGHT = ((0, 2), (2, 4), (4, 6), (6, 7))


def dot(a, b):
    return jnp.dot(a, b, preferred_element_type=F32)


def device(y, x, z, c):
    return ((y * 4 + x) * 2 + z // 4, (z % 4) * 2 + c)


def kernel(
    qkv_hbm, out_ref,
    qkv_ref, pieces, grouped, keys, doubled, values, queries, stationary, total, highest,
    part_out, stat_out, part_in, stat_in, back_out, back_in,
    a2a_s, a2a_r, kv_s, kv_r, q_s, q_r, po_s, po_r, bk_s, bk_r, in_sem,
):
    ctx, head = lax.axis_index("ctx"), lax.axis_index("head")
    y, x, z, c = ctx // 8, (ctx // 2) % 4, (ctx % 2) * 4 + head // 2, head % 2

    def y_peer(k):
        return device((y + k) % 8, x, z, c)

    def xc_peer(n):
        pair = n // 2
        dx = pair + pair // 2 - 2 * (pair // 3)
        return device(y, (x + dx) % 4, z, (c + n % 2) % 2)

    def inverse(n):
        pair = n // 2
        return 2 * ((2 * pair) % 3 + 3 * (pair // 3)) + n % 2

    left, right = device(y, x, (z + 7) % 8, c), device(y, x, (z + 1) % 8, c)

    barrier = pltpu.get_barrier_semaphore()
    partners = [y_peer(k) for k in range(1, 8)] + [xc_peer(n) for n in range(1, 8)] + [left, right]
    for partner in partners:
        pl.semaphore_signal(barrier, inc=1, device_id=partner, device_id_type=MESH)

    fetch = pltpu.make_async_copy(qkv_hbm, qkv_ref, in_sem)
    fetch.start()
    fetch.wait()

    for t in (1, 2, 0):
        for h in range(8):
            cut = qkv_ref[t, :, 64 * h : 64 * h + 64]
            pieces[h, t] = jnp.concatenate([cut[:32], cut[32:]], axis=1)

    pl.semaphore_wait(barrier, len(partners))

    def spread(k, first, count, part):
        there = (y + k) % 8
        return pltpu.make_async_remote_copy(
            src_ref=pieces.at[there, pl.ds(first, count)],
            dst_ref=grouped.at[pl.ds(first, count), y],
            send_sem=a2a_s.at[k, part],
            recv_sem=a2a_r.at[k, part],
            device_id=y_peer(k),
            device_id_type=MESH,
        )

    kv_spread = [spread(k, 1, 2, 0) for k in (4, 3, 5, 2, 6, 1, 7)]
    q_spread = [spread(k, 0, 1, 1) for k in (4, 3, 5, 2, 6, 1, 7)]
    for copy in kv_spread + q_spread:
        copy.start()
    for t in range(3):
        grouped[t, y] = pieces[y, t]
    for n in range(8):
        values[n, :, 64:80, :] = jnp.ones((2, 16, 256), BF16)
    started = kv_spread + q_spread

    def place(n, part):
        if part < 2:
            return keys.at[n, pl.ds(128 * part, 128)]
        return values.at[n, part - 2, pl.ds(0, 64)]

    def send_keys(step, part):
        copies = []
        for direction in range(2):
            if step < 3 or direction == part // 2:
                here, there = (KEY_LEFT, KEY_RIGHT)[direction][step]
                copies.append(
                    pltpu.make_async_remote_copy(
                        src_ref=place(here, part),
                        dst_ref=place(there, part),
                        send_sem=kv_s.at[step, direction, part],
                        recv_sem=kv_r.at[there, part],
                        device_id=(left, right)[direction],
                        device_id_type=MESH,
                    )
                )
        for copy in copies:
            copy.start()
        started.extend(copies)
        arriving[step, part] = copies

    arriving = {}

    def double_keys(n, part):
        both = keys[n, 128 * part : 128 * part + 128]
        for h in range(2):
            one = both[:, 64 * h : 64 * h + 64]
            doubled[n, h, 128 * part : 128 * part + 128] = jnp.concatenate([one, one], axis=1)

    def take_keys(step, *parts):
        for part in parts:
            for copy in arriving[step, part]:
                copy.wait_recv()
            if step < 3:
                send_keys(step + 1, part)
        for part in parts:
            if part < 2:
                for n in (1 + 2 * step, 2 + 2 * step)[: 2 if step < 3 else 1]:
                    double_keys(n, part)

    for copy in kv_spread:
        copy.wait_recv()
    keys[0] = grouped[1].reshape(256, 128)
    send_keys(0, 0)
    send_keys(0, 1)
    turned = grouped[2].reshape(256, 128).astype(F32).T.astype(BF16)
    values[0, 0, :64] = turned[:64]
    values[0, 1, :64] = turned[64:]
    send_keys(0, 2)
    send_keys(0, 3)
    double_keys(0, 0)
    double_keys(0, 1)

    for copy in q_spread:
        copy.wait_recv()
    queries[0] = grouped[0].reshape(256, 128).astype(F32).T.astype(BF16)

    q_copies = {}
    for n in (1, 2, 4, 3, 5, 6, 7):
        q_copies[n] = pltpu.make_async_remote_copy(
            src_ref=queries.at[0],
            dst_ref=queries.at[inverse(n)],
            send_sem=q_s.at[n],
            recv_sem=q_r.at[inverse(n)],
            device_id=xc_peer(n),
            device_id_type=MESH,
        )
        q_copies[n].start()
        started.append(q_copies[n])

    def take_queries(n):
        if n:
            q_copies[inverse(n)].wait_recv()
        scaled = queries[n].astype(F32) * (LOG2E / 8)
        high = scaled.astype(BF16)
        low = (scaled - high.astype(F32)).astype(BF16)
        for t in range(2):
            stationary[2 * n + t, :64, :] = high[64 * t : 64 * t + 64]
            stationary[2 * n + t, 64:, :] = low[64 * t : 64 * t + 64]

    def scores(i, n, h):
        found = [dot(doubled[n, h], stationary[2 * i + t]) for t in range(2)]
        return found, [jnp.max(s.reshape(32, 8, 256), axis=0) for s in found]

    state = {"chunk": None}

    def store():
        if state["chunk"] is not None:
            for t in range(2):
                top, whole = state["values"][t]
                highest[2 * state["chunk"] + t] = jnp.broadcast_to(top, (8, 256))
                total[2 * state["chunk"] + t] = whole

    def load(i, first):
        store()
        state["chunk"] = i
        state["values"] = [None if first else (highest[2 * i + t][:1], total[2 * i + t]) for t in range(2)]

    def weigh(i, n, h, found, top):
        if state["chunk"] != i:
            load(i, n == 0 and h == 0)
        for t in range(2):
            newest = jnp.max(top[t], axis=0, keepdims=True)
            if state["values"][t] is not None:
                before, whole = state["values"][t]
                newest = jnp.maximum(before, newest)
                factor = jnp.exp2(before - newest)
            added = dot(values[n, h], jnp.exp2(found[t] - newest).astype(BF16))
            state["values"][t] = (newest, added if state["values"][t] is None else whole * factor + added)
        if n == 7 and h == 1:
            give(i)

    held = []

    def attend(chunks, slots):
        for i in chunks:
            for n in slots:
                for h in range(2):
                    held.append((i, n, h, *scores(i, n, h)))
                    if len(held) > 2:
                        weigh(*held.pop(0))

    def finish_units():
        while held:
            weigh(*held.pop(0))

    def give_back(n):
        there = inverse(n)
        pairs = ((part_out, part_in), (stat_out, stat_in))
        return [
            pltpu.make_async_remote_copy(
                src_ref=mine.at[n],
                dst_ref=theirs.at[there],
                send_sem=po_s.at[n, k],
                recv_sem=po_r.at[there, k],
                device_id=xc_peer(n),
                device_id_type=MESH,
            )
            for k, (mine, theirs) in enumerate(pairs)
        ]

    def give(i):
        for t in range(2):
            top, whole = state["values"][t]
            sums = whole[64:65]
            part_out[i, 64 * t : 64 * t + 64, :] = (whole[:64] * (1.0 / sums)).astype(BF16)
            stat_out[i, 4 * t : 4 * t + 4, :] = jnp.broadcast_to(top + jnp.log2(sums), (4, 256))
        state["chunk"] = None
        if i:
            for copy in give_back(i):
                copy.start()

    take_queries(0)
    attend((0,), (0,))
    take_queries(1)
    attend((1,), (0,))
    take_keys(0, 0, 1, 2, 3)
    attend((0, 1), (1, 2))
    take_queries(2)
    take_queries(4)
    take_keys(1, 0)
    attend((2,), (0, 1, 2))
    take_keys(1, 1)
    attend((4,), (0, 1, 2))
    take_queries(3)
    take_queries(5)
    take_keys(1, 2)
    attend((3,), (0, 1, 2))
    take_keys(1, 3)
    attend((5,), (0, 1, 2))
    take_keys(2, 0)
    attend((0, 1), (3, 4))
    take_keys(2, 1)
    attend((2,), (3, 4))
    take_keys(2, 2)
    attend((3, 4), (3, 4))
    take_keys(2, 3)
    attend((5,), (3, 4))
    take_queries(6)
    take_queries(7)
    attend((6, 7), (0, 1, 2, 3, 4))
    take_keys(3, 0, 1, 2, 3)
    attend((6, 7, 2, 4, 3, 5, 0, 1), (5, 6, 7))
    finish_units()

    for n in range(1, 8):
        for copy in give_back(inverse(n)):
            copy.wait_recv()
    mixed = []
    for t in range(2):
        stats = [stat_out[0, 4 * t : 4 * t + 1, :]] + [stat_in[n, 4 * t : 4 * t + 1, :] for n in range(1, 8)]
        top = functools.reduce(jnp.maximum, stats)
        shares = [jnp.exp2(s - top) for s in stats]
        scale = 1.0 / sum(shares)
        piece = [part_out[0, 64 * t : 64 * t + 64, :]] + [part_in[n, 64 * t : 64 * t + 64, :] for n in range(1, 8)]
        mixed.append(sum(p.astype(F32) * (s * scale) for p, s in zip(piece, shares)))
    back_out[...] = jnp.concatenate(mixed, axis=0).T.astype(BF16).reshape(8, 32, 128)

    returns = []
    for k in (4, 3, 5, 2, 6, 1, 7):
        copy = pltpu.make_async_remote_copy(
            src_ref=back_out.at[(y + k) % 8],
            dst_ref=back_in.at[y],
            send_sem=bk_s.at[k],
            recv_sem=bk_r.at[k],
            device_id=y_peer(k),
            device_id_type=MESH,
        )
        copy.start()
        returns.append(copy)
    back_in[y] = back_out[y]
    for copy in started:
        copy.wait_send()
    for n in range(1, 8):
        for copy in give_back(n):
            copy.wait_send()
    for copy in returns:
        copy.wait_recv()
    for h in range(8):
        for t in range(2):
            out_ref[32 * t : 32 * t + 32, 64 * h : 64 * h + 64] = back_in[h][:, 64 * t : 64 * t + 64]
    for copy in returns:
        copy.wait_send()


def body(qkv, w_out):
    dma = pltpu.SemaphoreType.DMA
    attended = pl.pallas_call(
        kernel,
        out_shape=jax.ShapeDtypeStruct((64, 512), BF16),
        in_specs=[pl.BlockSpec(memory_space=pl.ANY)],
        out_specs=pl.BlockSpec(memory_space=pltpu.VMEM),
        scratch_shapes=[
            pltpu.VMEM((3, 64, 512), BF16),
            pltpu.VMEM((8, 3, 32, 128), BF16),
            pltpu.VMEM((3, 8, 32, 128), BF16),
            pltpu.VMEM((8, 256, 128), BF16),
            pltpu.VMEM((8, 2, 256, 128), BF16),
            pltpu.VMEM((8, 2, 80, 256), BF16),
            pltpu.VMEM((8, 128, 256), BF16),
            pltpu.VMEM((16, 128, 256), BF16),
            pltpu.VMEM((16, 80, 256), F32),
            pltpu.VMEM((16, 8, 256), F32),
            pltpu.VMEM((8, 128, 256), BF16),
            pltpu.VMEM((8, 8, 256), F32),
            pltpu.VMEM((8, 128, 256), BF16),
            pltpu.VMEM((8, 8, 256), F32),
            pltpu.VMEM((8, 32, 128), BF16),
            pltpu.VMEM((8, 32, 128), BF16),
            dma((8, 2)), dma((8, 2)),
            dma((4, 2, 4)), dma((8, 4)),
            dma((8,)), dma((8,)),
            dma((8, 2)), dma((8, 2)),
            dma((8,)), dma((8,)),
            dma,
        ],
        compiler_params=pltpu.CompilerParams(collective_id=0, has_side_effects=True, vmem_limit_bytes=56 << 20),
    )(qkv.transpose(1, 0, 2))
    return dot(attended, w_out).astype(BF16)


def solution(mesh):
    return jax.shard_map(
        body,
        mesh=mesh,
        in_specs=(P(("ctx", "head"), None, None), P()),
        out_specs=P(("ctx", "head"), None),
        check_vma=False,
    )
```

```python
import functools

import jax
import jax.numpy as jnp
from jax import lax
from jax.experimental import pallas as pl
from jax.experimental.pallas import tpu as pltpu
from jax.sharding import PartitionSpec as P

MESH = pl.DeviceIdType.MESH
F32 = jnp.float32
BF16 = jnp.bfloat16
LOG2E = 1.4426950408889634

KEY_LEFT = ((0, 1), (1, 3), (3, 5), (5, 7))
KEY_RIGHT = ((0, 2), (2, 4), (4, 6), (6, 7))


def dot(a, b):
    return jnp.dot(a, b, preferred_element_type=F32)


def device(y, x, z, c):
    return ((y * 4 + x) * 2 + z // 4, (z % 4) * 2 + c)


def kernel(
    qkv_hbm, out_ref,
    qkv_ref, pieces, grouped, keys, doubled, values, queries, stationary, total, highest,
    part_out, stat_out, part_in, stat_in, back_out, back_in,
    a2a_s, a2a_r, kv_s, kv_r, q_s, q_r, po_s, po_r, bk_s, bk_r, in_sem,
):
    ctx, head = lax.axis_index("ctx"), lax.axis_index("head")
    y, x, z, c = ctx // 8, (ctx // 2) % 4, (ctx % 2) * 4 + head // 2, head % 2

    def y_peer(k):
        return device((y + k) % 8, x, z, c)

    def xc_peer(n):
        pair = n // 2
        dx = pair + pair // 2 - 2 * (pair // 3)
        return device(y, (x + dx) % 4, z, (c + n % 2) % 2)

    def inverse(n):
        pair = n // 2
        return 2 * ((2 * pair) % 3 + 3 * (pair // 3)) + n % 2

    left, right = device(y, x, (z + 7) % 8, c), device(y, x, (z + 1) % 8, c)

    barrier = pltpu.get_barrier_semaphore()
    partners = [y_peer(k) for k in range(1, 8)] + [xc_peer(n) for n in range(1, 8)] + [left, right]
    for partner in partners:
        pl.semaphore_signal(barrier, inc=1, device_id=partner, device_id_type=MESH)

    fetch = pltpu.make_async_copy(qkv_hbm, qkv_ref, in_sem)
    fetch.start()
    fetch.wait()

    for t in (1, 2, 0):
        for h in range(8):
            cut = qkv_ref[t, :, 64 * h : 64 * h + 64]
            pieces[h, t] = jnp.concatenate([cut[:32], cut[32:]], axis=1)

    pl.semaphore_wait(barrier, len(partners))

    def spread(k, first, count, part):
        there = (y + k) % 8
        return pltpu.make_async_remote_copy(
            src_ref=pieces.at[there, pl.ds(first, count)],
            dst_ref=grouped.at[pl.ds(first, count), y],
            send_sem=a2a_s.at[k, part],
            recv_sem=a2a_r.at[k, part],
            device_id=y_peer(k),
            device_id_type=MESH,
        )

    kv_spread = [spread(k, 1, 2, 0) for k in (4, 3, 5, 2, 6, 1, 7)]
    q_spread = [spread(k, 0, 1, 1) for k in (4, 3, 5, 2, 6, 1, 7)]
    for copy in kv_spread + q_spread:
        copy.start()
    for t in range(3):
        grouped[t, y] = pieces[y, t]
    for n in range(8):
        values[n, :, 64:80, :] = jnp.ones((2, 16, 256), BF16)
    started = kv_spread + q_spread

    def place(n, part):
        if part < 2:
            return keys.at[n, pl.ds(128 * part, 128)]
        return values.at[n, part - 2, pl.ds(0, 64)]

    def send_keys(step, part, *directions):
        copies = []
        for direction in directions:
            if step < 3 or direction == part // 2:
                here, there = (KEY_LEFT, KEY_RIGHT)[direction][step]
                copies.append(
                    pltpu.make_async_remote_copy(
                        src_ref=place(here, part),
                        dst_ref=place(there, part),
                        send_sem=kv_s.at[step, direction, part],
                        recv_sem=kv_r.at[there, part],
                        device_id=(left, right)[direction],
                        device_id_type=MESH,
                    )
                )
        for copy in copies:
            copy.start()
        started.extend(copies)
        arriving[step, part] = arriving.get((step, part), []) + copies

    arriving = {}

    def double_keys(n, part):
        both = keys[n, 128 * part : 128 * part + 128]
        for h in range(2):
            one = both[:, 64 * h : 64 * h + 64]
            doubled[n, h, 128 * part : 128 * part + 128] = jnp.concatenate([one, one], axis=1)

    def take_keys(step, *parts):
        for part in parts:
            for direction, copy in enumerate(arriving[step, part]):
                copy.wait_recv()
                if step < 3:
                    send_keys(step + 1, part, direction)
        for part in parts:
            if part < 2:
                for n in (1 + 2 * step, 2 + 2 * step)[: 2 if step < 3 else 1]:
                    double_keys(n, part)

    for copy in kv_spread:
        copy.wait_recv()
    keys[0] = grouped[1].reshape(256, 128)
    send_keys(0, 0, 0, 1)
    send_keys(0, 1, 0, 1)
    turned = grouped[2].reshape(256, 128).astype(F32).T.astype(BF16)
    values[0, 0, :64] = turned[:64]
    values[0, 1, :64] = turned[64:]
    send_keys(0, 2, 0, 1)
    send_keys(0, 3, 0, 1)
    double_keys(0, 0)
    double_keys(0, 1)

    for copy in q_spread:
        copy.wait_recv()
    queries[0] = grouped[0].reshape(256, 128).astype(F32).T.astype(BF16)

    q_copies = {}
    for n in (1, 2, 4, 3, 5, 6, 7):
        q_copies[n] = pltpu.make_async_remote_copy(
            src_ref=queries.at[0],
            dst_ref=queries.at[inverse(n)],
            send_sem=q_s.at[n],
            recv_sem=q_r.at[inverse(n)],
            device_id=xc_peer(n),
            device_id_type=MESH,
        )
        q_copies[n].start()
        started.append(q_copies[n])

    def take_queries(n):
        if n:
            q_copies[inverse(n)].wait_recv()
        scaled = queries[n].astype(F32) * (LOG2E / 8)
        high = scaled.astype(BF16)
        low = (scaled - high.astype(F32)).astype(BF16)
        for t in range(2):
            stationary[2 * n + t, :64, :] = high[64 * t : 64 * t + 64]
            stationary[2 * n + t, 64:, :] = low[64 * t : 64 * t + 64]

    def scores(i, n, h):
        found = [dot(doubled[n, h], stationary[2 * i + t]) for t in range(2)]
        return found, [jnp.max(s.reshape(32, 8, 256), axis=0) for s in found]

    state = {"chunk": None}

    def store():
        if state["chunk"] is not None:
            for t in range(2):
                top, whole = state["values"][t]
                highest[2 * state["chunk"] + t] = jnp.broadcast_to(top, (8, 256))
                total[2 * state["chunk"] + t] = whole

    def load(i, first):
        store()
        state["chunk"] = i
        state["values"] = [None if first else (highest[2 * i + t][:1], total[2 * i + t]) for t in range(2)]

    def weigh(i, n, h, found, top):
        if state["chunk"] != i:
            load(i, n == 0 and h == 0)
        for t in range(2):
            newest = jnp.max(top[t], axis=0, keepdims=True)
            if state["values"][t] is not None:
                before, whole = state["values"][t]
                newest = jnp.maximum(before, newest)
                factor = jnp.exp2(before - newest)
            added = dot(values[n, h], jnp.exp2(found[t] - newest).astype(BF16))
            state["values"][t] = (newest, added if state["values"][t] is None else whole * factor + added)
        if n == 7 and h == 1:
            give(i)

    held = []

    def attend(chunks, slots):
        for i in chunks:
            for n in slots:
                for h in range(2):
                    held.append((i, n, h, *scores(i, n, h)))
                    if len(held) > 2:
                        weigh(*held.pop(0))

    def finish_units():
        while held:
            weigh(*held.pop(0))

    def give_back(n):
        there = inverse(n)
        pairs = ((part_out, part_in), (stat_out, stat_in))
        return [
            pltpu.make_async_remote_copy(
                src_ref=mine.at[n],
                dst_ref=theirs.at[there],
                send_sem=po_s.at[n, k],
                recv_sem=po_r.at[there, k],
                device_id=xc_peer(n),
                device_id_type=MESH,
            )
            for k, (mine, theirs) in enumerate(pairs)
        ]

    def give(i):
        for t in range(2):
            top, whole = state["values"][t]
            sums = whole[64:65]
            part_out[i, 64 * t : 64 * t + 64, :] = (whole[:64] * (1.0 / sums)).astype(BF16)
            stat = top + jnp.log2(sums)
            for k in range(2):
                row = 4 * t + 2 * k
                stat_out[i, row : row + 2, :] = jnp.broadcast_to(stat[:, 128 * k : 128 * k + 128], (2, 128))
        state["chunk"] = None
        if i:
            for copy in give_back(i):
                copy.start()

    take_queries(0)
    attend((0,), (0,))
    take_queries(1)
    attend((1,), (0,))
    take_keys(0, 0, 1, 2, 3)
    attend((0, 1), (1, 2))
    take_queries(2)
    take_queries(4)
    take_keys(1, 0)
    attend((2,), (0, 1, 2))
    take_keys(1, 1)
    attend((4,), (0, 1, 2))
    take_queries(3)
    take_queries(5)
    take_keys(1, 2)
    attend((3,), (0, 1, 2))
    take_keys(1, 3)
    attend((5,), (0, 1, 2))
    take_keys(2, 0)
    attend((0, 1), (3, 4))
    take_keys(2, 1)
    attend((2,), (3, 4))
    take_keys(2, 2)
    attend((3, 4), (3, 4))
    take_keys(2, 3)
    attend((5,), (3, 4))
    take_queries(6)
    take_queries(7)
    attend((6, 7), (0, 1, 2, 3, 4))
    take_keys(3, 0, 1, 2, 3)
    attend((6, 7, 2, 4, 3, 5, 0, 1), (5, 6, 7))
    finish_units()

    for n in range(1, 8):
        for copy in give_back(inverse(n)):
            copy.wait_recv()
    mixed = []
    for t in range(2):
        stats = [
            jnp.concatenate([ref[n, 4 * t + 2 * k : 4 * t + 2 * k + 1, :] for k in range(2)], axis=1)
            for n, ref in enumerate([stat_out] + 7 * [stat_in])
        ]
        top = functools.reduce(jnp.maximum, stats)
        shares = [jnp.exp2(s - top) for s in stats]
        scale = 1.0 / sum(shares)
        piece = [part_out[0, 64 * t : 64 * t + 64, :]] + [part_in[n, 64 * t : 64 * t + 64, :] for n in range(1, 8)]
        mixed.append(sum(p.astype(F32) * (s * scale) for p, s in zip(piece, shares)))
    back_out[...] = jnp.concatenate(mixed, axis=0).T.astype(BF16).reshape(8, 32, 128)

    returns = []
    for k in (4, 3, 5, 2, 6, 1, 7):
        copy = pltpu.make_async_remote_copy(
            src_ref=back_out.at[(y + k) % 8],
            dst_ref=back_in.at[y],
            send_sem=bk_s.at[k],
            recv_sem=bk_r.at[k],
            device_id=y_peer(k),
            device_id_type=MESH,
        )
        copy.start()
        returns.append(copy)
    back_in[y] = back_out[y]
    for copy in started:
        copy.wait_send()
    for n in range(1, 8):
        for copy in give_back(n):
            copy.wait_send()
    for copy in returns:
        copy.wait_recv()
    for h in range(8):
        for t in range(2):
            out_ref[32 * t : 32 * t + 32, 64 * h : 64 * h + 64] = back_in[h][:, 64 * t : 64 * t + 64]
    for copy in returns:
        copy.wait_send()


def body(qkv, w_out):
    dma = pltpu.SemaphoreType.DMA
    attended = pl.pallas_call(
        kernel,
        out_shape=jax.ShapeDtypeStruct((64, 512), BF16),
        in_specs=[pl.BlockSpec(memory_space=pl.ANY)],
        out_specs=pl.BlockSpec(memory_space=pltpu.VMEM),
        scratch_shapes=[
            pltpu.VMEM((3, 64, 512), BF16),
            pltpu.VMEM((8, 3, 32, 128), BF16),
            pltpu.VMEM((3, 8, 32, 128), BF16),
            pltpu.VMEM((8, 256, 128), BF16),
            pltpu.VMEM((8, 2, 256, 128), BF16),
            pltpu.VMEM((8, 2, 80, 256), BF16),
            pltpu.VMEM((8, 128, 256), BF16),
            pltpu.VMEM((16, 128, 256), BF16),
            pltpu.VMEM((16, 80, 256), F32),
            pltpu.VMEM((16, 8, 256), F32),
            pltpu.VMEM((8, 128, 256), BF16),
            pltpu.VMEM((8, 8, 128), F32),
            pltpu.VMEM((8, 128, 256), BF16),
            pltpu.VMEM((8, 8, 128), F32),
            pltpu.VMEM((8, 32, 128), BF16),
            pltpu.VMEM((8, 32, 128), BF16),
            dma((8, 2)), dma((8, 2)),
            dma((4, 2, 4)), dma((8, 4)),
            dma((8,)), dma((8,)),
            dma((8, 2)), dma((8, 2)),
            dma((8,)), dma((8,)),
            dma,
        ],
        compiler_params=pltpu.CompilerParams(collective_id=0, has_side_effects=True, vmem_limit_bytes=56 << 20),
    )(qkv.transpose(1, 0, 2))
    return dot(attended, w_out).astype(BF16)


def solution(mesh):
    return jax.shard_map(
        body,
        mesh=mesh,
        in_specs=(P(("ctx", "head"), None, None), P()),
        out_specs=P(("ctx", "head"), None),
        check_vma=False,
    )
```

```python
import functools

import jax
import jax.numpy as jnp
from jax import lax
from jax.experimental import pallas as pl
from jax.experimental.pallas import tpu as pltpu
from jax.sharding import PartitionSpec as P

MESH = pl.DeviceIdType.MESH
F32 = jnp.float32
BF16 = jnp.bfloat16
LOG2E = 1.4426950408889634

KEY_LEFT = ((0, 1), (1, 3), (3, 5), (5, 7))
KEY_RIGHT = ((0, 2), (2, 4), (4, 6), (6, 7))


def dot(a, b):
    return jnp.dot(a, b, preferred_element_type=F32)


def device(y, x, z, c):
    return ((y * 4 + x) * 2 + z // 4, (z % 4) * 2 + c)


def kernel(
    qkv_hbm, out_ref,
    qkv_ref, pieces, grouped, keys, doubled, values, queries, stationary, total, highest,
    part_out, stat_out, part_in, stat_in, back_out, back_in,
    a2a_s, a2a_r, kv_s, kv_r, q_s, q_r, po_s, po_r, bk_s, bk_r, in_sem,
):
    ctx, head = lax.axis_index("ctx"), lax.axis_index("head")
    y, x, z, c = ctx // 8, (ctx // 2) % 4, (ctx % 2) * 4 + head // 2, head % 2

    def y_peer(k):
        return device((y + k) % 8, x, z, c)

    def xc_peer(n):
        pair = n // 2
        dx = pair + pair // 2 - 2 * (pair // 3)
        return device(y, (x + dx) % 4, z, (c + n % 2) % 2)

    def inverse(n):
        pair = n // 2
        return 2 * ((2 * pair) % 3 + 3 * (pair // 3)) + n % 2

    left, right = device(y, x, (z + 7) % 8, c), device(y, x, (z + 1) % 8, c)

    barrier = pltpu.get_barrier_semaphore()
    partners = [y_peer(k) for k in range(1, 8)] + [xc_peer(n) for n in range(1, 8)] + [left, right]
    for partner in partners:
        pl.semaphore_signal(barrier, inc=1, device_id=partner, device_id_type=MESH)

    fetch = pltpu.make_async_copy(qkv_hbm, qkv_ref, in_sem)
    fetch.start()
    fetch.wait()

    def cut_pieces(t):
        for h in range(8):
            cut = qkv_ref[t, :, 64 * h : 64 * h + 64]
            pieces[h, t] = jnp.concatenate([cut[:32], cut[32:]], axis=1)

    cut_pieces(1)
    cut_pieces(2)
    pl.semaphore_wait(barrier, len(partners))

    def spread(k, first, count, part):
        there = (y + k) % 8
        return pltpu.make_async_remote_copy(
            src_ref=pieces.at[there, pl.ds(first, count)],
            dst_ref=grouped.at[pl.ds(first, count), y],
            send_sem=a2a_s.at[k, part],
            recv_sem=a2a_r.at[k, part],
            device_id=y_peer(k),
            device_id_type=MESH,
        )

    kv_spread = [spread(k, 1, 2, 0) for k in (4, 3, 5, 2, 6, 1, 7)]
    q_spread = [spread(k, 0, 1, 1) for k in (4, 3, 5, 2, 6, 1, 7)]
    for copy in kv_spread:
        copy.start()
    cut_pieces(0)
    for copy in q_spread:
        copy.start()
    for t in range(3):
        grouped[t, y] = pieces[y, t]
    for n in range(8):
        values[n, :, 64:80, :] = jnp.ones((2, 16, 256), BF16)
    started = kv_spread + q_spread

    def place(n, part):
        if part < 2:
            return keys.at[n, pl.ds(128 * part, 128)]
        return values.at[n, part - 2, pl.ds(0, 64)]

    def send_keys(step, part, *directions):
        copies = []
        for direction in directions:
            if step < 3 or direction == part // 2:
                here, there = (KEY_LEFT, KEY_RIGHT)[direction][step]
                copies.append(
                    pltpu.make_async_remote_copy(
                        src_ref=place(here, part),
                        dst_ref=place(there, part),
                        send_sem=kv_s.at[step, direction, part],
                        recv_sem=kv_r.at[there, part],
                        device_id=(left, right)[direction],
                        device_id_type=MESH,
                    )
                )
        for copy in copies:
            copy.start()
        started.extend(copies)
        arriving[step, part] = arriving.get((step, part), []) + copies

    arriving = {}

    def double_keys(n, part):
        both = keys[n, 128 * part : 128 * part + 128]
        for h in range(2):
            one = both[:, 64 * h : 64 * h + 64]
            doubled[n, h, 128 * part : 128 * part + 128] = jnp.concatenate([one, one], axis=1)

    def take_keys(step, *parts):
        for part in parts:
            for direction, copy in enumerate(arriving[step, part]):
                copy.wait_recv()
                if step < 3:
                    send_keys(step + 1, part, direction)
        for part in parts:
            if part < 2:
                for n in (1 + 2 * step, 2 + 2 * step)[: 2 if step < 3 else 1]:
                    double_keys(n, part)

    for copy in kv_spread:
        copy.wait_recv()
    keys[0] = grouped[1].reshape(256, 128)
    send_keys(0, 0, 0, 1)
    send_keys(0, 1, 0, 1)
    turned = grouped[2].reshape(256, 128).astype(F32).T.astype(BF16)
    values[0, 0, :64] = turned[:64]
    values[0, 1, :64] = turned[64:]
    send_keys(0, 2, 0, 1)
    send_keys(0, 3, 0, 1)
    double_keys(0, 0)
    double_keys(0, 1)

    for copy in q_spread:
        copy.wait_recv()
    queries[0] = grouped[0].reshape(256, 128).astype(F32).T.astype(BF16)

    q_copies = {}
    for n in (1, 2, 4, 3, 5, 6, 7):
        q_copies[n] = pltpu.make_async_remote_copy(
            src_ref=queries.at[0],
            dst_ref=queries.at[inverse(n)],
            send_sem=q_s.at[n],
            recv_sem=q_r.at[inverse(n)],
            device_id=xc_peer(n),
            device_id_type=MESH,
        )
        q_copies[n].start()
        started.append(q_copies[n])

    def take_queries(n):
        if n:
            q_copies[inverse(n)].wait_recv()
        scaled = queries[n].astype(F32) * (LOG2E / 8)
        high = scaled.astype(BF16)
        low = (scaled - high.astype(F32)).astype(BF16)
        for t in range(2):
            stationary[2 * n + t, :64, :] = high[64 * t : 64 * t + 64]
            stationary[2 * n + t, 64:, :] = low[64 * t : 64 * t + 64]

    def scores(i, n, h):
        found = [dot(doubled[n, h], stationary[2 * i + t]) for t in range(2)]
        return found, [jnp.max(s.reshape(32, 8, 256), axis=0) for s in found]

    state = {"chunk": None}

    def store():
        if state["chunk"] is not None:
            for t in range(2):
                top, whole = state["values"][t]
                highest[2 * state["chunk"] + t] = jnp.broadcast_to(top, (8, 256))
                total[2 * state["chunk"] + t] = whole

    def load(i, first):
        store()
        state["chunk"] = i
        state["values"] = [None if first else (highest[2 * i + t][:1], total[2 * i + t]) for t in range(2)]

    def weigh(i, n, h, found, top):
        if state["chunk"] != i:
            load(i, n == 0 and h == 0)
        for t in range(2):
            newest = jnp.max(top[t], axis=0, keepdims=True)
            if state["values"][t] is not None:
                before, whole = state["values"][t]
                newest = jnp.maximum(before, newest)
                factor = jnp.exp2(before - newest)
            added = dot(values[n, h], jnp.exp2(found[t] - newest).astype(BF16))
            state["values"][t] = (newest, added if state["values"][t] is None else whole * factor + added)
        if n == 7 and h == 1:
            give(i)

    held = []

    def attend(chunks, slots):
        for i in chunks:
            for n in slots:
                for h in range(2):
                    held.append((i, n, h, *scores(i, n, h)))
                    if len(held) > 2:
                        weigh(*held.pop(0))

    def finish_units():
        while held:
            weigh(*held.pop(0))

    def give_back(n):
        there = inverse(n)
        pairs = ((part_out, part_in), (stat_out, stat_in))
        return [
            pltpu.make_async_remote_copy(
                src_ref=mine.at[n],
                dst_ref=theirs.at[there],
                send_sem=po_s.at[n, k],
                recv_sem=po_r.at[there, k],
                device_id=xc_peer(n),
                device_id_type=MESH,
            )
            for k, (mine, theirs) in enumerate(pairs)
        ]

    def give(i):
        for t in range(2):
            top, whole = state["values"][t]
            sums = whole[64:65]
            part_out[i, 64 * t : 64 * t + 64, :] = (whole[:64] * (1.0 / sums)).astype(BF16)
            stat = top + jnp.log2(sums)
            for k in range(2):
                row = 4 * t + 2 * k
                stat_out[i, row : row + 2, :] = jnp.broadcast_to(stat[:, 128 * k : 128 * k + 128], (2, 128))
        state["chunk"] = None
        if i:
            for copy in give_back(i):
                copy.start()

    take_queries(0)
    attend((0,), (0,))
    take_queries(1)
    attend((1,), (0,))
    take_keys(0, 0, 1, 2, 3)
    attend((0, 1), (1, 2))
    take_queries(2)
    take_queries(4)
    take_keys(1, 0)
    attend((2,), (0, 1, 2))
    take_keys(1, 1)
    attend((4,), (0, 1, 2))
    take_queries(3)
    take_queries(5)
    take_keys(1, 2)
    attend((3,), (0, 1, 2))
    take_keys(1, 3)
    attend((5,), (0, 1, 2))
    take_keys(2, 0)
    attend((0, 1), (3, 4))
    take_keys(2, 1)
    attend((2,), (3, 4))
    take_keys(2, 2)
    attend((3, 4), (3, 4))
    take_keys(2, 3)
    attend((5,), (3, 4))
    take_queries(6)
    take_queries(7)
    attend((6, 7), (0, 1, 2, 3, 4))
    take_keys(3, 0, 1, 2, 3)
    attend((6, 7, 2, 4, 3, 5, 0, 1), (5, 6, 7))
    finish_units()

    merged = []
    for n in (0, 1, 6, 7, 4, 2, 5, 3):
        if n:
            for copy in give_back(inverse(n)):
                copy.wait_recv()
        part, stat = (part_in, stat_in) if n else (part_out, stat_out)
        for t in range(2):
            size = jnp.concatenate([stat[n, 4 * t + 2 * k : 4 * t + 2 * k + 1, :] for k in range(2)], axis=1)
            piece = part[n, 64 * t : 64 * t + 64, :].astype(F32)
            if n == 0:
                merged.append((size, jnp.ones_like(size), piece))
            else:
                top, share, whole = merged[t]
                newest = jnp.maximum(top, size)
                old, new = jnp.exp2(top - newest), jnp.exp2(size - newest)
                merged[t] = (newest, share * old + new, whole * old + piece * new)
    mixed = [whole * (1.0 / share) for top, share, whole in merged]
    back_out[...] = jnp.concatenate(mixed, axis=0).T.astype(BF16).reshape(8, 32, 128)

    returns = []
    for k in (4, 3, 5, 2, 6, 1, 7):
        copy = pltpu.make_async_remote_copy(
            src_ref=back_out.at[(y + k) % 8],
            dst_ref=back_in.at[y],
            send_sem=bk_s.at[k],
            recv_sem=bk_r.at[k],
            device_id=y_peer(k),
            device_id_type=MESH,
        )
        copy.start()
        returns.append(copy)
    back_in[y] = back_out[y]
    for copy in started:
        copy.wait_send()
    for n in range(1, 8):
        for copy in give_back(n):
            copy.wait_send()
    for copy in returns:
        copy.wait_recv()
    for h in range(8):
        for t in range(2):
            out_ref[32 * t : 32 * t + 32, 64 * h : 64 * h + 64] = back_in[h][:, 64 * t : 64 * t + 64]
    for copy in returns:
        copy.wait_send()


def body(qkv, w_out):
    dma = pltpu.SemaphoreType.DMA
    attended = pl.pallas_call(
        kernel,
        out_shape=jax.ShapeDtypeStruct((64, 512), BF16),
        in_specs=[pl.BlockSpec(memory_space=pl.ANY)],
        out_specs=pl.BlockSpec(memory_space=pltpu.VMEM),
        scratch_shapes=[
            pltpu.VMEM((3, 64, 512), BF16),
            pltpu.VMEM((8, 3, 32, 128), BF16),
            pltpu.VMEM((3, 8, 32, 128), BF16),
            pltpu.VMEM((8, 256, 128), BF16),
            pltpu.VMEM((8, 2, 256, 128), BF16),
            pltpu.VMEM((8, 2, 80, 256), BF16),
            pltpu.VMEM((8, 128, 256), BF16),
            pltpu.VMEM((16, 128, 256), BF16),
            pltpu.VMEM((16, 80, 256), F32),
            pltpu.VMEM((16, 8, 256), F32),
            pltpu.VMEM((8, 128, 256), BF16),
            pltpu.VMEM((8, 8, 128), F32),
            pltpu.VMEM((8, 128, 256), BF16),
            pltpu.VMEM((8, 8, 128), F32),
            pltpu.VMEM((8, 32, 128), BF16),
            pltpu.VMEM((8, 32, 128), BF16),
            dma((8, 2)), dma((8, 2)),
            dma((4, 2, 4)), dma((8, 4)),
            dma((8,)), dma((8,)),
            dma((8, 2)), dma((8, 2)),
            dma((8,)), dma((8,)),
            dma,
        ],
        compiler_params=pltpu.CompilerParams(collective_id=0, has_side_effects=True, vmem_limit_bytes=56 << 20),
    )(qkv.transpose(1, 0, 2))
    return dot(attended, w_out).astype(BF16)


def solution(mesh):
    return jax.shard_map(
        body,
        mesh=mesh,
        in_specs=(P(("ctx", "head"), None, None), P()),
        out_specs=P(("ctx", "head"), None),
        check_vma=False,
    )
```

```python
import functools

import jax
import jax.numpy as jnp
from jax import lax
from jax.experimental import pallas as pl
from jax.experimental.pallas import tpu as pltpu
from jax.sharding import PartitionSpec as P

MESH = pl.DeviceIdType.MESH
F32 = jnp.float32
BF16 = jnp.bfloat16
LOG2E = 1.4426950408889634

KEY_LEFT = ((0, 1), (1, 3), (3, 5), (5, 7))
KEY_RIGHT = ((0, 2), (2, 4), (4, 6), (6, 7))


def dot(a, b):
    return jnp.dot(a, b, preferred_element_type=F32)


def device(y, x, z, c):
    return ((y * 4 + x) * 2 + z // 4, (z % 4) * 2 + c)


def kernel(
    qkv_hbm, out_ref,
    qkv_ref, pieces, grouped, keys, doubled, values, queries, stationary, total, highest,
    part_out, stat_out, part_in, stat_in, back_out, back_in,
    a2a_s, a2a_r, kv_s, kv_r, q_s, q_r, po_s, po_r, bk_s, bk_r, in_sem,
):
    ctx, head = lax.axis_index("ctx"), lax.axis_index("head")
    y, x, z, c = ctx // 8, (ctx // 2) % 4, (ctx % 2) * 4 + head // 2, head % 2

    def y_peer(k):
        return device((y + k) % 8, x, z, c)

    def xc_peer(n):
        pair = n // 2
        dx = pair + pair // 2 - 2 * (pair // 3)
        return device(y, (x + dx) % 4, z, (c + n % 2) % 2)

    def inverse(n):
        pair = n // 2
        return 2 * ((2 * pair) % 3 + 3 * (pair // 3)) + n % 2

    left, right = device(y, x, (z + 7) % 8, c), device(y, x, (z + 1) % 8, c)

    barrier = pltpu.get_barrier_semaphore()
    partners = [y_peer(k) for k in range(1, 8)] + [xc_peer(n) for n in range(1, 8)] + [left, right]
    for partner in partners:
        pl.semaphore_signal(barrier, inc=1, device_id=partner, device_id_type=MESH)

    fetch = pltpu.make_async_copy(qkv_hbm, qkv_ref, in_sem)
    fetch.start()
    fetch.wait()

    def cut_pieces(t):
        for h in range(8):
            cut = qkv_ref[t, :, 64 * h : 64 * h + 64]
            pieces[h, t] = jnp.concatenate([cut[:32], cut[32:]], axis=1)

    cut_pieces(1)
    cut_pieces(2)
    pl.semaphore_wait(barrier, len(partners))

    def spread(k, first, count, part):
        there = (y + k) % 8
        return pltpu.make_async_remote_copy(
            src_ref=pieces.at[there, pl.ds(first, count)],
            dst_ref=grouped.at[pl.ds(first, count), y],
            send_sem=a2a_s.at[k, part],
            recv_sem=a2a_r.at[k, part],
            device_id=y_peer(k),
            device_id_type=MESH,
        )

    k_spread = [spread(k, 1, 1, 0) for k in (4, 3, 5, 2, 6, 1, 7)]
    v_spread = [spread(k, 2, 1, 2) for k in (4, 3, 5, 2, 6, 1, 7)]
    q_spread = [spread(k, 0, 1, 1) for k in (4, 3, 5, 2, 6, 1, 7)]
    for copy in k_spread + v_spread:
        copy.start()
    cut_pieces(0)
    for copy in q_spread:
        copy.start()
    for t in range(3):
        grouped[t, y] = pieces[y, t]
    for n in range(8):
        values[n, :, 64:80, :] = jnp.ones((2, 16, 256), BF16)
    started = k_spread + v_spread + q_spread

    def place(n, part):
        if part < 2:
            return keys.at[n, pl.ds(128 * part, 128)]
        return values.at[n, part - 2, pl.ds(0, 64)]

    def send_keys(step, part, *directions):
        copies = []
        for direction in directions:
            if step < 3 or direction == part // 2:
                here, there = (KEY_LEFT, KEY_RIGHT)[direction][step]
                copies.append(
                    pltpu.make_async_remote_copy(
                        src_ref=place(here, part),
                        dst_ref=place(there, part),
                        send_sem=kv_s.at[step, direction, part],
                        recv_sem=kv_r.at[there, part],
                        device_id=(left, right)[direction],
                        device_id_type=MESH,
                    )
                )
        for copy in copies:
            copy.start()
        started.extend(copies)
        arriving[step, part] = arriving.get((step, part), []) + copies

    arriving = {}

    def double_keys(n, part):
        both = keys[n, 128 * part : 128 * part + 128]
        for h in range(2):
            one = both[:, 64 * h : 64 * h + 64]
            doubled[n, h, 128 * part : 128 * part + 128] = jnp.concatenate([one, one], axis=1)

    def take_keys(step, *parts):
        for part in parts:
            for direction, copy in enumerate(arriving[step, part]):
                copy.wait_recv()
                if step < 3:
                    send_keys(step + 1, part, direction)
        for part in parts:
            if part < 2:
                for n in (1 + 2 * step, 2 + 2 * step)[: 2 if step < 3 else 1]:
                    double_keys(n, part)

    for copy in k_spread:
        copy.wait_recv()
    keys[0] = grouped[1].reshape(256, 128)
    send_keys(0, 0, 0, 1)
    send_keys(0, 1, 0, 1)
    for copy in v_spread:
        copy.wait_recv()
    turned = grouped[2].reshape(256, 128).astype(F32).T.astype(BF16)
    values[0, 0, :64] = turned[:64]
    values[0, 1, :64] = turned[64:]
    send_keys(0, 2, 0, 1)
    send_keys(0, 3, 0, 1)
    double_keys(0, 0)
    double_keys(0, 1)

    for copy in q_spread:
        copy.wait_recv()
    queries[0] = grouped[0].reshape(256, 128).astype(F32).T.astype(BF16)

    q_copies = {}
    for n in (1, 2, 4, 3, 5, 6, 7):
        q_copies[n] = pltpu.make_async_remote_copy(
            src_ref=queries.at[0],
            dst_ref=queries.at[inverse(n)],
            send_sem=q_s.at[n],
            recv_sem=q_r.at[inverse(n)],
            device_id=xc_peer(n),
            device_id_type=MESH,
        )
        q_copies[n].start()
        started.append(q_copies[n])

    def take_queries(n):
        if n:
            q_copies[inverse(n)].wait_recv()
        scaled = queries[n].astype(F32) * (LOG2E / 8)
        high = scaled.astype(BF16)
        low = (scaled - high.astype(F32)).astype(BF16)
        for t in range(2):
            stationary[2 * n + t, :64, :] = high[64 * t : 64 * t + 64]
            stationary[2 * n + t, 64:, :] = low[64 * t : 64 * t + 64]

    def scores(i, n, h):
        found = [dot(doubled[n, h], stationary[2 * i + t]) for t in range(2)]
        return found, [jnp.max(s.reshape(32, 8, 256), axis=0) for s in found]

    state = {"chunk": None}

    def store():
        if state["chunk"] is not None:
            for t in range(2):
                top, whole = state["values"][t]
                highest[2 * state["chunk"] + t] = jnp.broadcast_to(top, (8, 256))
                total[2 * state["chunk"] + t] = whole

    def load(i, first):
        store()
        state["chunk"] = i
        state["values"] = [None if first else (highest[2 * i + t][:1], total[2 * i + t]) for t in range(2)]

    def weigh(i, n, h, found, top):
        if state["chunk"] != i:
            load(i, n == 0 and h == 0)
        for t in range(2):
            newest = jnp.max(top[t], axis=0, keepdims=True)
            if state["values"][t] is not None:
                before, whole = state["values"][t]
                newest = jnp.maximum(before, newest)
                factor = jnp.exp2(before - newest)
            added = dot(values[n, h], jnp.exp2(found[t] - newest).astype(BF16))
            state["values"][t] = (newest, added if state["values"][t] is None else whole * factor + added)
        if n == 7 and h == 1:
            give(i)

    held = []

    def attend(chunks, slots):
        for i in chunks:
            for n in slots:
                for h in range(2):
                    held.append((i, n, h, *scores(i, n, h)))
                    if len(held) > 2:
                        weigh(*held.pop(0))

    def finish_units():
        while held:
            weigh(*held.pop(0))

    def give_back(n):
        there = inverse(n)
        pairs = ((part_out, part_in), (stat_out, stat_in))
        return [
            pltpu.make_async_remote_copy(
                src_ref=mine.at[n],
                dst_ref=theirs.at[there],
                send_sem=po_s.at[n, k],
                recv_sem=po_r.at[there, k],
                device_id=xc_peer(n),
                device_id_type=MESH,
            )
            for k, (mine, theirs) in enumerate(pairs)
        ]

    def give(i):
        for t in range(2):
            top, whole = state["values"][t]
            sums = whole[64:65]
            part_out[i, 64 * t : 64 * t + 64, :] = (whole[:64] * (1.0 / sums)).astype(BF16)
            stat = top + jnp.log2(sums)
            for k in range(2):
                row = 4 * t + 2 * k
                stat_out[i, row : row + 2, :] = jnp.broadcast_to(stat[:, 128 * k : 128 * k + 128], (2, 128))
        state["chunk"] = None
        if i:
            for copy in give_back(i):
                copy.start()

    take_queries(0)
    attend((0,), (0,))
    take_queries(1)
    attend((1,), (0,))
    take_keys(0, 0, 1, 2, 3)
    attend((0, 1), (1, 2))
    take_queries(2)
    take_queries(4)
    take_keys(1, 0)
    attend((2,), (0, 1, 2))
    take_keys(1, 1)
    attend((4,), (0, 1, 2))
    take_queries(3)
    take_queries(5)
    take_keys(1, 2)
    attend((3,), (0, 1, 2))
    take_keys(1, 3)
    attend((5,), (0, 1, 2))
    take_keys(2, 0)
    attend((0, 1), (3, 4))
    take_keys(2, 1)
    attend((2,), (3, 4))
    take_keys(2, 2)
    attend((3, 4), (3, 4))
    take_keys(2, 3)
    attend((5,), (3, 4))
    take_queries(6)
    take_queries(7)
    attend((6, 7), (0, 1, 2, 3, 4))
    take_keys(3, 0, 1, 2, 3)
    attend((6, 7, 2, 4, 3, 5, 0, 1), (5, 6, 7))
    finish_units()

    merged = []
    for n in (0, 1, 6, 7, 4, 2, 5, 3):
        if n:
            for copy in give_back(inverse(n)):
                copy.wait_recv()
        part, stat = (part_in, stat_in) if n else (part_out, stat_out)
        for t in range(2):
            size = jnp.concatenate([stat[n, 4 * t + 2 * k : 4 * t + 2 * k + 1, :] for k in range(2)], axis=1)
            piece = part[n, 64 * t : 64 * t + 64, :].astype(F32)
            if n == 0:
                merged.append((size, jnp.ones_like(size), piece))
            else:
                top, share, whole = merged[t]
                newest = jnp.maximum(top, size)
                old, new = jnp.exp2(top - newest), jnp.exp2(size - newest)
                merged[t] = (newest, share * old + new, whole * old + piece * new)
    mixed = [whole * (1.0 / share) for top, share, whole in merged]
    back_out[...] = jnp.concatenate(mixed, axis=0).T.astype(BF16).reshape(8, 32, 128)

    returns = []
    for k in (4, 3, 5, 2, 6, 1, 7):
        copy = pltpu.make_async_remote_copy(
            src_ref=back_out.at[(y + k) % 8],
            dst_ref=back_in.at[y],
            send_sem=bk_s.at[k],
            recv_sem=bk_r.at[k],
            device_id=y_peer(k),
            device_id_type=MESH,
        )
        copy.start()
        returns.append(copy)
    back_in[y] = back_out[y]
    for copy in started:
        copy.wait_send()
    for n in range(1, 8):
        for copy in give_back(n):
            copy.wait_send()
    for copy in returns:
        copy.wait_recv()
    for h in range(8):
        for t in range(2):
            out_ref[32 * t : 32 * t + 32, 64 * h : 64 * h + 64] = back_in[h][:, 64 * t : 64 * t + 64]
    for copy in returns:
        copy.wait_send()


def body(qkv, w_out):
    dma = pltpu.SemaphoreType.DMA
    attended = pl.pallas_call(
        kernel,
        out_shape=jax.ShapeDtypeStruct((64, 512), BF16),
        in_specs=[pl.BlockSpec(memory_space=pl.ANY)],
        out_specs=pl.BlockSpec(memory_space=pltpu.VMEM),
        scratch_shapes=[
            pltpu.VMEM((3, 64, 512), BF16),
            pltpu.VMEM((8, 3, 32, 128), BF16),
            pltpu.VMEM((3, 8, 32, 128), BF16),
            pltpu.VMEM((8, 256, 128), BF16),
            pltpu.VMEM((8, 2, 256, 128), BF16),
            pltpu.VMEM((8, 2, 80, 256), BF16),
            pltpu.VMEM((8, 128, 256), BF16),
            pltpu.VMEM((16, 128, 256), BF16),
            pltpu.VMEM((16, 80, 256), F32),
            pltpu.VMEM((16, 8, 256), F32),
            pltpu.VMEM((8, 128, 256), BF16),
            pltpu.VMEM((8, 8, 128), F32),
            pltpu.VMEM((8, 128, 256), BF16),
            pltpu.VMEM((8, 8, 128), F32),
            pltpu.VMEM((8, 32, 128), BF16),
            pltpu.VMEM((8, 32, 128), BF16),
            dma((8, 3)), dma((8, 3)),
            dma((4, 2, 4)), dma((8, 4)),
            dma((8,)), dma((8,)),
            dma((8, 2)), dma((8, 2)),
            dma((8,)), dma((8,)),
            dma,
        ],
        compiler_params=pltpu.CompilerParams(collective_id=0, has_side_effects=True, vmem_limit_bytes=56 << 20),
    )(qkv.transpose(1, 0, 2))
    return dot(attended, w_out).astype(BF16)


def solution(mesh):
    return jax.shard_map(
        body,
        mesh=mesh,
        in_specs=(P(("ctx", "head"), None, None), P()),
        out_specs=P(("ctx", "head"), None),
        check_vma=False,
    )
```
